32 devices in a mesh: sta: 8 (over y, x, core), tm: 4 (over z).
Axes of the slice: x: 2, y: 2, z: 4, core: 2. Of those that a mesh axis runs over, the one named last changes fastest.
Arguments:
- strain: bfloat16 [256, 4096], P('sta', 'tm'), may hold values from -1800 to 1800
- plan: int32 [4], replicated, may hold values from 1 to 7, as said below
Outputs:
- correlations: float32 [4096, 1024], P('tm', 'sta')
The draws below stay inside these ranges and needn't reach their ends.
Inputs may be any that keep to these rules, and one draw needn't show every extreme that they name: In round r block b is paired with block b XOR plan[r]; the 4 keys are distinct, and every draw holds the keys 1 and 7.
All inputs are finite; a program needn't handle non-finite values.
Results may differ from the reference program's by a relative error of at most 0.0041.
Values may be sent and summed in bfloat16 or wider, within the bound.
No kernel may reach another device: no remote copies, remote signals or barrier semaphores. Data moves between devices by JAX's collectives and lax.ppermute only.
A program may use at most 192 MiB of HBM per device.

```python
import math
import jax
import jax.numpy as jnp
from jax import lax

CH_DEV = 32
SOURCES = 4
MAX_LAG = 512
ROUNDS = 4
LAGS = 1024
BLOCKS = 8
CHANNELS = 256
SPAN_LENGTH = 4096


def draw_strain(key, part):
    noise_key, random_seed_state, channel_key = jax.random.split(key, 3)
    position = jnp.arange(SPAN_LENGTH, dtype=jnp.float32)[None, :] / SPAN_LENGTH
    background_strain_record = jnp.clip(jax.random.normal(noise_key, (CHANNELS, SPAN_LENGTH), jnp.float32), -6.0, 6.0)
    expansion_multiplier = jnp.exp(position * math.log(3.0))
    transient_pulses = jnp.exp(jax.random.uniform(random_seed_state, (1, SPAN_LENGTH), jnp.float32, 0.0, math.log(10.0)))
    amplitude_scaling = jnp.exp(jax.random.uniform(channel_key, (CHANNELS, 1), jnp.float32, 0.0, math.log(10.0)))
    return (background_strain_record * transient_pulses * amplitude_scaling * expansion_multiplier).astype(jnp.bfloat16)


def draw_plan(key, part):
    middle = jax.random.permutation(key, jnp.arange(2, BLOCKS - 1, dtype=jnp.int32))[:ROUNDS - 2]
    picked = jnp.concatenate([jnp.array([1, BLOCKS - 1], dtype=jnp.int32), middle])
    return jax.random.permutation(jax.random.fold_in(key, 7), picked)


def setup_inputs(seed: int = 0) -> dict:
    keys = jax.random.split(jax.random.key(seed), 3)
    return {
        "strain": draw_strain(jax.random.fold_in(keys[2], 71), 0),
        "plan": draw_plan(jax.random.fold_in(keys[2], 71), 0),
    }


epsilon = 1e-06

def reference(strain, plan):
    widened = strain.astype(jnp.float32)
    energy = lax.optimization_barrier(jnp.mean(widened * widened, axis=1, keepdims=True))
    whitened = (widened * lax.rsqrt(energy + epsilon)).astype(jnp.bfloat16)
    per_block = whitened.astype(jnp.float32).reshape(BLOCKS, CH_DEV, SPAN_LENGTH)
    sources = per_block.reshape(BLOCKS, SOURCES, CH_DEV // SOURCES, SPAN_LENGTH)[:, :, 0, :]
    fft_len = 2 * SPAN_LENGTH
    spectra = jnp.fft.rfft(per_block, n=fft_len, axis=-1)
    source_spec = jnp.fft.rfft(sources, n=fft_len, axis=-1)
    block_ids = jnp.arange(BLOCKS, dtype=jnp.int32)
    per_round = []
    for round_index in range(ROUNDS):
        paired_block = jnp.bitwise_xor(block_ids, plan[round_index])
        mate_spec = source_spec[paired_block]
        per_source = []
        for source_index in range(SOURCES):
            circular = jnp.fft.irfft(spectra * jnp.conj(mate_spec[:, source_index:source_index + 1, :]), n=fft_len, axis=-1)
            per_source.append(jnp.concatenate([circular[..., fft_len - MAX_LAG:], circular[..., :MAX_LAG]], axis=-1))
        per_round.append(jnp.stack(per_source))
    assembled = jnp.stack(per_round) / math.sqrt(SPAN_LENGTH)
    return jnp.transpose(assembled, (1, 4, 2, 3, 0)).reshape(SOURCES * LAGS, CHANNELS * ROUNDS)
```

```python
import functools
import math

import jax
import jax.numpy as jnp
from jax import lax
from jax.experimental import pallas as pl
from jax.experimental.pallas import tpu as pltpu
from jax.sharding import PartitionSpec as P

SOURCES = 4
MAX_LAG = 512
ROUNDS = 4
LAGS = 1024
WIDTH = 128

epsilon = 1e-06


def swap(block, axis, key):
    count = lax.axis_size(axis)
    return lax.ppermute(block, axis, [(i, i ^ key) for i in range(count)])


def place(base, step, index):
    return pl.multiple_of(base + step * index, 128)


def fill_shifts(line, shifts, round_index):
    length = line.shape[1]
    shape = (WIDTH, 128)
    mask = lax.broadcasted_iota(jnp.int32, shape, 1) >= lax.broadcasted_iota(jnp.int32, shape, 0)
    rows = pl.ds(round_index * WIDTH, WIDTH)

    def body(q, before):
        piece = line[round_index : round_index + 1, pl.ds(place(0, 128, q), 128)]
        now = pltpu.roll(jnp.broadcast_to(piece, shape), 0, 1, stride=1, stride_axis=0)
        shifts[rows, pl.ds(place(0, 128, q), 128)] = jnp.where(mask, now, before).astype(jnp.bfloat16)
        return now

    last = lax.fori_loop(0, length // 128, body, jnp.zeros(shape, jnp.float32), unroll=4)
    shifts[rows, length : length + 128] = jnp.where(mask, 0.0, last).astype(jnp.bfloat16)


def kernel(tiles, groups, plan, *refs):
    strain, mates = refs[:tiles], refs[tiles : tiles + groups]
    out, wide, mate, line, shifts, stacked, total, turned, mate_scale = refs[tiles + groups :]
    channels, tile_len = strain[0].shape
    length = tiles * tile_len
    depth = length + WIDTH
    row_count = out.shape[0]
    blocks = row_count // WIDTH
    here = lax.axis_index("tm")
    low_lag = 0 if row_count == LAGS else lax.rem(here * row_count, LAGS)

    wide[:, :MAX_LAG] = jnp.zeros((channels, MAX_LAG), jnp.bfloat16)
    wide[:, MAX_LAG + length :] = jnp.zeros((channels, MAX_LAG + WIDTH), jnp.bfloat16)
    squares = jnp.zeros((channels, 1), jnp.float32)
    for k in range(tiles):
        wide[:, pl.ds(place(MAX_LAG, tile_len, here ^ k), tile_len)] = strain[k][...]
        widened = strain[k][...].astype(jnp.float32)
        squares += jnp.sum(widened * widened, axis=1, keepdims=True)
        for g in range(groups):
            mate[2 * g : 2 * g + 2, pl.ds(place(0, tile_len, here ^ k), tile_len)] = mates[g][
                :, k * tile_len : (k + 1) * tile_len
            ].astype(jnp.float32)
    scale = lax.rsqrt(squares / length + epsilon) * (1.0 / math.sqrt(length))
    squares = jnp.sum(mate[...] * mate[...], axis=1, keepdims=True)
    mate_scale[...] = jnp.broadcast_to(lax.rsqrt(squares / length + epsilon), mate_scale.shape)

    for r in range(ROUNDS):
        line[r : r + 1, :] = mate[pl.ds(plan[r], 1), :]
        fill_shifts(line, shifts, r)
    for j in range(blocks):
        stacked[channels * j : channels * (j + 1), :] = wide[
            :, pl.ds(place(WIDTH * j, 1, low_lag), depth)
        ]
    total[...] = lax.dot_general(
        stacked[...], shifts[...], (((1,), (1,)), ((), ())), preferred_element_type=jnp.float32
    )
    for j in range(blocks):
        for r in range(ROUNDS):
            both = scale * mate_scale[pl.ds(plan[r], 1), :]
            turned[j % 2, pl.ds(r, channels, stride=ROUNDS), :] = (
                total[channels * j : channels * (j + 1), WIDTH * r : WIDTH * (r + 1)] * both
            )
        out[WIDTH * j : WIDTH * (j + 1), :] = turned[j % 2].T


def correlate(plan, strain, mates, row_count):
    tiles, groups = len(strain), len(mates)
    channels, tile_len = strain[0].shape
    length = tiles * tile_len
    depth = length + WIDTH
    stacked_rows = channels * row_count // WIDTH
    in_vmem = pl.BlockSpec(memory_space=pltpu.VMEM)
    return pl.pallas_call(
        functools.partial(kernel, tiles, groups),
        out_shape=jax.ShapeDtypeStruct((row_count, channels * ROUNDS), jnp.float32),
        in_specs=[pl.BlockSpec(memory_space=pltpu.SMEM)] + [in_vmem] * (tiles + groups),
        out_specs=in_vmem,
        scratch_shapes=[
            pltpu.VMEM((channels, length + 2 * MAX_LAG + WIDTH), jnp.bfloat16),
            pltpu.VMEM((2 * groups, length), jnp.float32),
            pltpu.VMEM((8, length), jnp.float32),
            pltpu.VMEM((ROUNDS * WIDTH, depth), jnp.bfloat16),
            pltpu.VMEM((stacked_rows, depth), jnp.bfloat16),
            pltpu.VMEM((stacked_rows, ROUNDS * WIDTH), jnp.float32),
            pltpu.VMEM((2, channels * ROUNDS, WIDTH), jnp.float32),
            pltpu.VMEM((2 * groups, WIDTH), jnp.float32),
        ],
        compiler_params=pltpu.CompilerParams(vmem_limit_bytes=40 * 2**20),
    )(plan, *strain, *mates)


def local(strain, plan):
    tile_count, block_count = lax.axis_size("tm"), lax.axis_size("sta")
    row_count = SOURCES * LAGS // tile_count
    source = lax.axis_index("tm") * row_count // LAGS
    tiles = [strain] + [swap(strain, "tm", k) for k in range(1, tile_count)]
    row = source * (strain.shape[0] // SOURCES)
    own = jnp.concatenate([lax.dynamic_slice_in_dim(tile, row, 1, 0) for tile in tiles], axis=1)
    pair = jnp.concatenate([own, swap(own, "sta", 1)])
    mates = [pair] + [swap(pair, "sta", 2 * g) for g in range(1, block_count // 2)]
    return correlate(plan, tiles, mates, row_count)


def solution(mesh):
    in_specs = (P("sta", "tm"), P())
    out_specs = P("tm", "sta")
    return jax.shard_map(local, mesh=mesh, in_specs=in_specs, out_specs=out_specs, check_vma=False)
```

```python
import functools
import math

import jax
import jax.numpy as jnp
from jax import lax
from jax.experimental import pallas as pl
from jax.experimental.pallas import tpu as pltpu
from jax.sharding import PartitionSpec as P

SOURCES = 4
MAX_LAG = 512
ROUNDS = 4
LAGS = 1024
WIDTH = 128

epsilon = 1e-06


def swap(block, axis, key):
    count = lax.axis_size(axis)
    return lax.ppermute(block, axis, [(i, i ^ key) for i in range(count)])


def place(base, step, index):
    if isinstance(index, int):
        return base + step * index
    return pl.multiple_of(base + step * index, 128)


def fill_shifts(line, shifts):
    length = line.shape[1]
    shape = (WIDTH, 128)
    mask = lax.broadcasted_iota(jnp.int32, shape, 1) >= lax.broadcasted_iota(jnp.int32, shape, 0)
    pieces = math.gcd(length // 128, 32)

    for r in range(ROUNDS):
        rows = slice(r * WIDTH, (r + 1) * WIDTH)

        def body(step, before):
            for q in range(pieces):
                at = pl.ds(place(128 * q, 128 * pieces, step), 128)
                piece = jnp.broadcast_to(line[r : r + 1, at], shape)
                now = pltpu.roll(piece, 0, 1, stride=1, stride_axis=0)
                shifts[rows, at] = jnp.where(mask, now, before).astype(jnp.bfloat16)
                before = now
            return before

        steps = length // (128 * pieces)
        zero = jnp.zeros(shape, jnp.float32)
        last = body(0, zero) if steps == 1 else lax.fori_loop(0, steps, body, zero)
        shifts[rows, length : length + 128] = jnp.where(mask, 0.0, last).astype(jnp.bfloat16)


def kernel(tiles, groups, plan, *refs):
    strain, mates = refs[:tiles], refs[tiles : tiles + groups]
    out, wide, mate, line, shifts, stacked, total, turned = refs[tiles + groups :]
    channels, tile_len = strain[0].shape
    length = tiles * tile_len
    depth = length + WIDTH
    row_count = out.shape[0]
    blocks = row_count // WIDTH
    here = lax.axis_index("tm")
    low_lag = 0 if row_count == LAGS else lax.rem(here * row_count, LAGS)

    wide[:, :MAX_LAG] = jnp.zeros((channels, MAX_LAG), jnp.bfloat16)
    wide[:, MAX_LAG + length :] = jnp.zeros((channels, MAX_LAG + WIDTH), jnp.bfloat16)
    squares = jnp.zeros((channels, 1), jnp.float32)
    for k in range(tiles):
        widened = strain[k][...].astype(jnp.float32)
        squares += jnp.sum(widened * widened, axis=1, keepdims=True)
        for g in range(groups):
            mate[2 * g : 2 * g + 2, pl.ds(place(0, tile_len, here ^ k), tile_len)] = mates[g][
                :, k * tile_len : (k + 1) * tile_len
            ].astype(jnp.float32)
    scale = lax.rsqrt(squares / length + epsilon)
    for k in range(tiles):
        wide[:, pl.ds(place(MAX_LAG, tile_len, here ^ k), tile_len)] = (
            strain[k][...].astype(jnp.float32) * scale
        ).astype(jnp.bfloat16)
    for r in range(ROUNDS):
        line[r : r + 1, :] = mate[pl.ds(plan[r], 1), :]
    squares = jnp.sum(line[...] * line[...], axis=1, keepdims=True)
    line[...] = (line[...] * lax.rsqrt(squares / length + epsilon)).astype(jnp.bfloat16).astype(jnp.float32)
    fill_shifts(line, shifts)
    for j in range(blocks):
        stacked[channels * j : channels * (j + 1), :] = wide[
            :, pl.ds(place(WIDTH * j, 1, low_lag), depth)
        ]
    total[...] = lax.dot_general(
        stacked[...], shifts[...], (((1,), (1,)), ((), ())), preferred_element_type=jnp.float32
    )
    for j in range(blocks):
        for r in range(ROUNDS):
            turned[j % 2, pl.ds(r, channels, stride=ROUNDS), :] = total[
                channels * j : channels * (j + 1), WIDTH * r : WIDTH * (r + 1)
            ]
        out[WIDTH * j : WIDTH * (j + 1), :] = turned[j % 2].T * (1.0 / math.sqrt(length))


def correlate(plan, strain, mates, row_count):
    tiles, groups = len(strain), len(mates)
    channels, tile_len = strain[0].shape
    length = tiles * tile_len
    depth = length + WIDTH
    stacked_rows = channels * row_count // WIDTH
    in_vmem = pl.BlockSpec(memory_space=pltpu.VMEM)
    return pl.pallas_call(
        functools.partial(kernel, tiles, groups),
        out_shape=jax.ShapeDtypeStruct((row_count, channels * ROUNDS), jnp.float32),
        in_specs=[pl.BlockSpec(memory_space=pltpu.SMEM)] + [in_vmem] * (tiles + groups),
        out_specs=in_vmem,
        scratch_shapes=[
            pltpu.VMEM((channels, length + 2 * MAX_LAG + WIDTH), jnp.bfloat16),
            pltpu.VMEM((2 * groups, length), jnp.float32),
            pltpu.VMEM((ROUNDS, length), jnp.float32),
            pltpu.VMEM((ROUNDS * WIDTH, depth), jnp.bfloat16),
            pltpu.VMEM((stacked_rows, depth), jnp.bfloat16),
            pltpu.VMEM((stacked_rows, ROUNDS * WIDTH), jnp.float32),
            pltpu.VMEM((2, channels * ROUNDS, WIDTH), jnp.float32),
        ],
        compiler_params=pltpu.CompilerParams(vmem_limit_bytes=40 * 2**20),
    )(plan, *strain, *mates)


def local(strain, plan):
    tile_count, block_count = lax.axis_size("tm"), lax.axis_size("sta")
    row_count = SOURCES * LAGS // tile_count
    source = lax.axis_index("tm") * row_count // LAGS
    tiles = [strain] + [swap(strain, "tm", k) for k in range(1, tile_count)]
    row = source * (strain.shape[0] // SOURCES)
    own = jnp.concatenate([lax.dynamic_slice_in_dim(tile, row, 1, 0) for tile in tiles], axis=1)
    pair = jnp.concatenate([own, swap(own, "sta", 1)])
    mates = [pair] + [swap(pair, "sta", 2 * g) for g in range(1, block_count // 2)]
    return correlate(plan, tiles, mates, row_count)


def solution(mesh):
    in_specs = (P("sta", "tm"), P())
    out_specs = P("tm", "sta")
    return jax.shard_map(local, mesh=mesh, in_specs=in_specs, out_specs=out_specs, check_vma=False)
```

```python
import functools
import itertools
import math

import jax
import jax.numpy as jnp
from jax import lax
from jax.experimental import pallas as pl
from jax.experimental.pallas import tpu as pltpu
from jax.sharding import PartitionSpec as P

SOURCES = 4
MAX_LAG = 512
ROUNDS = 4
LAGS = 1024
WIDTH = 64
HALVES = 128 // WIDTH
MOST_BRANCHES = 16

epsilon = 1e-06


def swap(block, axis, key):
    count = lax.axis_size(axis)
    return lax.ppermute(block, axis, [(i, i ^ key) for i in range(count)])


def place(base, step, index):
    if isinstance(index, int):
        return base + step * index
    return pl.multiple_of(base + step * index, 128)


def stack_strain(keys, strain, stacked, wide):
    channels, tile_len = strain[0].shape
    length = len(keys) * tile_len
    blocks = stacked.shape[0] // channels
    here = lax.axis_index("tm")
    row_count = blocks * WIDTH
    low_lag = 0 if row_count == LAGS else lax.rem(here * row_count, LAGS)

    wide[0][:, :MAX_LAG] = jnp.zeros((channels, MAX_LAG), jnp.bfloat16)
    wide[0][:, MAX_LAG + length :] = jnp.zeros((channels, MAX_LAG + 128), jnp.bfloat16)
    squares = jnp.zeros((channels, 1), jnp.float32)
    for tile in strain:
        widened = tile[...].astype(jnp.float32)
        squares += jnp.sum(widened * widened, axis=1, keepdims=True)
    scale = lax.rsqrt(squares / length + epsilon)
    for key, tile in zip(keys, strain):
        wide[0][:, pl.ds(place(MAX_LAG, tile_len, here ^ key), tile_len)] = (
            tile[...].astype(jnp.float32) * scale
        ).astype(jnp.bfloat16)
    for half in range(1, HALVES):
        kept = wide[half].shape[1]
        wide[half][...] = wide[0][:, WIDTH * half : WIDTH * half + kept]
    for j in range(blocks):
        stacked[channels * j : channels * (j + 1), :] = wide[j % HALVES][
            :, pl.ds(place(128 * (j // HALVES), 1, low_lag), stacked.shape[1])
        ]


def fill_shifts(line, shifts):
    length = line.shape[1]
    shape = (WIDTH, 128)
    mask = lax.broadcasted_iota(jnp.int32, shape, 1) >= lax.broadcasted_iota(jnp.int32, shape, 0)
    pieces = math.gcd(length // 128, 32)

    for r in range(ROUNDS):
        rows = slice(r * WIDTH, (r + 1) * WIDTH)

        def body(step, before):
            for q in range(pieces):
                at = pl.ds(place(128 * q, 128 * pieces, step), 128)
                piece = jnp.broadcast_to(line[r : r + 1, at], shape)
                now = pltpu.roll(piece, 0, 1, stride=1, stride_axis=0)
                shifts[rows, at] = jnp.where(mask, now, before).astype(jnp.bfloat16)
                before = now
            return before

        steps = length // (128 * pieces)
        zero = jnp.zeros(shape, jnp.float32)
        last = body(0, zero) if steps == 1 else lax.fori_loop(0, steps, body, zero)
        shifts[rows, length : length + 128] = jnp.where(mask, 0.0, last).astype(jnp.bfloat16)


def correlate_kernel(keys, groups, chosen_far, *refs):
    tiles = len(keys)
    strain, far, (out, *refs) = refs[:tiles], refs[tiles : tiles + groups], refs[tiles + groups :]
    mates, refs = refs[:groups], refs[groups:]
    chosen, mate, line, stacked, shifts, total, turned, ready, fetched, sent, *wide = refs
    row_count = out.shape[0]
    channels, tile_len = strain[0].shape
    length = line.shape[1]
    here = lax.axis_index("tm")

    copies = [pltpu.make_async_copy(far[g], mates[g], fetched.at[g]) for g in range(groups)]
    copies.append(pltpu.make_async_copy(chosen_far, chosen, fetched.at[groups]))
    for copy in copies:
        copy.start()
    stack_strain(keys, strain, stacked, wide)
    for copy in copies:
        copy.wait()
    at = 0
    for group in mates:
        count = group.shape[0]
        for k, key in enumerate(keys):
            mate[at : at + count, pl.ds(place(0, tile_len, here ^ key), tile_len)] = group[
                :, k * tile_len : (k + 1) * tile_len
            ].astype(jnp.float32)
        at += count
    for r in range(ROUNDS):
        line[r : r + 1, :] = mate[pl.ds(chosen[r], 1), :]
    squares = jnp.sum(line[...] * line[...], axis=1, keepdims=True)
    whitened = line[...] * lax.rsqrt(squares / length + epsilon)
    line[...] = whitened.astype(jnp.bfloat16).astype(jnp.float32)
    fill_shifts(line, shifts)
    total[...] = lax.dot_general(
        stacked[...], shifts[...], (((1,), (1,)), ((), ())), preferred_element_type=jnp.float32
    )
    copies = []
    lane = lax.broadcasted_iota(jnp.int32, (channels, 128), 1)
    for block in range(row_count // 128):
        for r in range(ROUNDS):
            value = jnp.zeros((channels, 128), jnp.float32)
            for half in range(HALVES):
                rows = slice((block * HALVES + half) * channels, (block * HALVES + half + 1) * channels)
                first = WIDTH * r // 128 * 128
                part = total[rows, first : first + 128]
                if WIDTH * half != WIDTH * r - first:
                    part = pltpu.roll(part, (WIDTH * half - WIDTH * r + first) % 128, 1)
                value = part if half == 0 else jnp.where(lane >= WIDTH * half, part, value)
            turned[block % 2, pl.ds(r, channels, stride=ROUNDS), :] = value
        lags = slice(128 * block, 128 * (block + 1))
        ready[lags, :] = turned[block % 2].T * (1.0 / math.sqrt(length))
        copies.append(pltpu.make_async_copy(ready.at[lags], out.at[lags], sent.at[block]))
        copies[-1].start()
    for copy in copies:
        copy.wait()


def correlate(keys, chosen, strain, mates, row_count):
    channels, tile_len = strain[0].shape
    length = len(keys) * tile_len
    depth = length + 128
    stacked_rows = channels * row_count // WIDTH
    mate_rows = sum(group.shape[0] for group in mates)
    in_vmem = pl.BlockSpec(memory_space=pltpu.VMEM)
    anywhere = pl.BlockSpec(memory_space=pl.ANY)
    widths = [length + 2 * MAX_LAG + 128] + [length + 2 * MAX_LAG] * (HALVES - 1)
    return pl.pallas_call(
        functools.partial(correlate_kernel, keys, len(mates)),
        out_shape=jax.ShapeDtypeStruct((row_count, channels * ROUNDS), jnp.float32),
        in_specs=[anywhere]
        + [in_vmem] * len(strain)
        + [anywhere] * len(mates),
        out_specs=pl.BlockSpec(memory_space=pltpu.HBM),
        scratch_shapes=[
            *(pltpu.VMEM(group.shape, jnp.bfloat16) for group in mates),
            pltpu.SMEM(chosen.shape, jnp.int32),
            pltpu.VMEM((mate_rows, length), jnp.float32),
            pltpu.VMEM((ROUNDS, length), jnp.float32),
            pltpu.VMEM((stacked_rows, depth), jnp.bfloat16),
            pltpu.VMEM((ROUNDS * WIDTH, depth), jnp.bfloat16),
            pltpu.VMEM((stacked_rows, ROUNDS * WIDTH), jnp.float32),
            pltpu.VMEM((2, channels * ROUNDS, 128), jnp.float32),
            pltpu.VMEM((row_count, channels * ROUNDS), jnp.float32),
            pltpu.SemaphoreType.DMA((len(mates) + 1,)),
            pltpu.SemaphoreType.DMA((row_count // 128,)),
            *(pltpu.VMEM((channels, width), jnp.bfloat16) for width in widths),
        ],
        compiler_params=pltpu.CompilerParams(vmem_limit_bytes=40 * 2**20),
    )(chosen, *strain, *mates)


def by_plan(plan, own):
    block_count = lax.axis_size("sta")
    middle = range(2, block_count - 1)
    choices = list(itertools.combinations(middle, ROUNDS - 2))
    ends = (plan == 1) | (plan == block_count - 1)
    high = jnp.max(jnp.where(ends, 0, plan))
    low = jnp.min(jnp.where(ends, block_count, plan))
    first, span = low - 2, 2 * len(middle) - 1
    index = ((first * (span - first)) >> 1) + high - low - 1

    def branch(keys):
        return lambda own: jnp.concatenate([swap(own, "sta", key) for key in keys])

    branches = [branch((1, *keys, block_count - 1)) for keys in choices]
    ranks = jnp.sum((plan[None, :] < plan[:, None]).astype(jnp.int32), axis=1)
    index, ranks = lax.optimization_barrier((index, ranks))
    return ranks, lax.switch(index, branches, own)


def local(strain, plan):
    tile_count, block_count = lax.axis_size("tm"), lax.axis_size("sta")
    row_count = SOURCES * LAGS // tile_count
    source = lax.axis_index("tm") * row_count // LAGS
    order = sorted(range(tile_count), key=lambda k: (k > 1, k if k < 2 else -k))
    tiles = [strain] + [swap(strain, "tm", k) for k in order[1:]]
    row = source * (strain.shape[0] // SOURCES)
    own = jnp.concatenate([lax.dynamic_slice_in_dim(tile, row, 1, 0) for tile in tiles], axis=1)
    if math.comb(max(block_count - 3, 0), ROUNDS - 2) in range(1, MOST_BRANCHES + 1):
        chosen, mates = by_plan(plan, own)
        mates = [mates]
    else:
        chosen = plan
        pair = jnp.concatenate([own, swap(own, "sta", 1)])
        mates = [pair] + [swap(pair, "sta", 2 * g) for g in range(1, block_count // 2)]
    return correlate(order, chosen, tiles, mates, row_count)


def solution(mesh):
    in_specs = (P("sta", "tm"), P())
    out_specs = P("tm", "sta")
    return jax.shard_map(local, mesh=mesh, in_specs=in_specs, out_specs=out_specs, check_vma=False)
```

```python
import functools
import itertools
import math

import jax
import jax.numpy as jnp
from jax import lax
from jax.experimental import pallas as pl
from jax.experimental.pallas import tpu as pltpu
from jax.sharding import PartitionSpec as P

SOURCES = 4
MAX_LAG = 512
ROUNDS = 4
LAGS = 1024
WIDTH = 64
HALVES = 128 // WIDTH
MOST_BLOCKS = 8

epsilon = 1e-06


def swap(block, axis, key):
    count = lax.axis_size(axis)
    return lax.ppermute(block, axis, [(i, i ^ key) for i in range(count)])


def place(base, step, index):
    if isinstance(index, int):
        return base + step * index
    return pl.multiple_of(base + step * index, 128)


def stack_strain(keys, strain, stacked, wide):
    channels, tile_len = wide[0].shape[0], strain[0].shape[1]
    length = len(keys) * tile_len
    strain = [group.at[at : at + channels] for group in strain for at in range(0, group.shape[0], channels)]
    blocks = stacked.shape[0] // channels
    here = lax.axis_index("tm")
    row_count = blocks * WIDTH
    low_lag = 0 if row_count == LAGS else lax.rem(here * row_count, LAGS)

    wide[0][:, :MAX_LAG] = jnp.zeros((channels, MAX_LAG), jnp.bfloat16)
    wide[0][:, MAX_LAG + length :] = jnp.zeros((channels, MAX_LAG + 128), jnp.bfloat16)
    squares = jnp.zeros((channels, 1), jnp.float32)
    for tile in strain:
        widened = tile[...].astype(jnp.float32)
        squares += jnp.sum(widened * widened, axis=1, keepdims=True)
    scale = lax.rsqrt(squares / length + epsilon)
    for key, tile in zip(keys, strain):
        wide[0][:, pl.ds(place(MAX_LAG, tile_len, here ^ key), tile_len)] = (
            tile[...].astype(jnp.float32) * scale
        ).astype(jnp.bfloat16)
    for half in range(1, HALVES):
        kept = wide[half].shape[1]
        wide[half][...] = wide[0][:, WIDTH * half : WIDTH * half + kept]
    for j in range(blocks):
        stacked[channels * j : channels * (j + 1), :] = wide[j % HALVES][
            :, pl.ds(place(128 * (j // HALVES), 1, low_lag), stacked.shape[1])
        ]


def fill_shifts(line, shifts):
    length = line.shape[1]
    shape = (WIDTH, 128)
    mask = lax.broadcasted_iota(jnp.int32, shape, 1) >= lax.broadcasted_iota(jnp.int32, shape, 0)
    pieces = math.gcd(length // 128, 32)

    for r in range(ROUNDS):
        rows = slice(r * WIDTH, (r + 1) * WIDTH)

        def body(step, before):
            for q in range(pieces):
                at = pl.ds(place(128 * q, 128 * pieces, step), 128)
                piece = jnp.broadcast_to(line[r : r + 1, at], shape)
                now = pltpu.roll(piece, 0, 1, stride=1, stride_axis=0)
                shifts[rows, at] = jnp.where(mask, now, before).astype(jnp.bfloat16)
                before = now
            return before

        steps = length // (128 * pieces)
        zero = jnp.zeros(shape, jnp.float32)
        last = body(0, zero) if steps == 1 else lax.fori_loop(0, steps, body, zero)
        shifts[rows, length : length + 128] = jnp.where(mask, 0.0, last).astype(jnp.bfloat16)


def correlate_kernel(keys, row_keys, tiles, groups, chosen_far, *refs):
    strain, far, (out, *refs) = refs[:tiles], refs[tiles : tiles + groups], refs[tiles + groups :]
    mates, refs = refs[:groups], refs[groups:]
    chosen, mate, line, stacked, shifts, total, turned, ready, fetched, sent, *wide = refs
    row_count = out.shape[0]
    channels, tile_len = out.shape[1] // ROUNDS, strain[0].shape[1]
    length = line.shape[1]
    here = lax.axis_index("tm")

    copies = [pltpu.make_async_copy(far[g], mates[g], fetched.at[g]) for g in range(groups)]
    copies.append(pltpu.make_async_copy(chosen_far, chosen, fetched.at[groups]))
    for copy in copies:
        copy.start()
    stack_strain(keys, strain, stacked, wide)
    for copy in copies:
        copy.wait()
    at = 0
    for group in mates:
        count = group.shape[0]
        for k, key in enumerate(row_keys):
            mate[at : at + count, pl.ds(place(0, tile_len, here ^ key), tile_len)] = group[
                :, k * tile_len : (k + 1) * tile_len
            ].astype(jnp.float32)
        at += count
    for r in range(ROUNDS):
        line[r : r + 1, :] = mate[pl.ds(chosen[r], 1), :]
    squares = jnp.sum(line[...] * line[...], axis=1, keepdims=True)
    whitened = line[...] * lax.rsqrt(squares / length + epsilon)
    line[...] = whitened.astype(jnp.bfloat16).astype(jnp.float32)
    fill_shifts(line, shifts)
    total[...] = lax.dot_general(
        stacked[...], shifts[...], (((1,), (1,)), ((), ())), preferred_element_type=jnp.float32
    )
    copies = []
    lane = lax.broadcasted_iota(jnp.int32, (channels, 128), 1)
    for block in range(row_count // 128):
        for r in range(ROUNDS):
            value = jnp.zeros((channels, 128), jnp.float32)
            for half in range(HALVES):
                rows = slice((block * HALVES + half) * channels, (block * HALVES + half + 1) * channels)
                first = WIDTH * r // 128 * 128
                part = total[rows, first : first + 128]
                if WIDTH * half != WIDTH * r - first:
                    part = pltpu.roll(part, (WIDTH * half - WIDTH * r + first) % 128, 1)
                value = part if half == 0 else jnp.where(lane >= WIDTH * half, part, value)
            turned[block % 2, pl.ds(r, channels, stride=ROUNDS), :] = value
        lags = slice(128 * block, 128 * (block + 1))
        ready[lags, :] = turned[block % 2].T * (1.0 / math.sqrt(length))
        copies.append(pltpu.make_async_copy(ready.at[lags], out.at[lags], sent.at[block]))
        copies[-1].start()
    for copy in copies:
        copy.wait()


def correlate(keys, row_keys, chosen, strain, mates, row_count):
    rows, tile_len = strain[0].shape
    channels = rows * len(strain) // len(keys)
    length = len(keys) * tile_len
    depth = length + 128
    stacked_rows = channels * row_count // WIDTH
    mate_rows = sum(group.shape[0] for group in mates)
    in_vmem = pl.BlockSpec(memory_space=pltpu.VMEM)
    anywhere = pl.BlockSpec(memory_space=pl.ANY)
    widths = [length + 2 * MAX_LAG + 128] + [length + 2 * MAX_LAG] * (HALVES - 1)
    return pl.pallas_call(
        functools.partial(correlate_kernel, keys, row_keys, len(strain), len(mates)),
        out_shape=jax.ShapeDtypeStruct((row_count, channels * ROUNDS), jnp.float32),
        in_specs=[anywhere]
        + [in_vmem] * len(strain)
        + [anywhere] * len(mates),
        out_specs=pl.BlockSpec(memory_space=pltpu.HBM),
        scratch_shapes=[
            *(pltpu.VMEM(group.shape, jnp.bfloat16) for group in mates),
            pltpu.SMEM(chosen.shape, jnp.int32),
            pltpu.VMEM((mate_rows, length), jnp.float32),
            pltpu.VMEM((ROUNDS, length), jnp.float32),
            pltpu.VMEM((stacked_rows, depth), jnp.bfloat16),
            pltpu.VMEM((ROUNDS * WIDTH, depth), jnp.bfloat16),
            pltpu.VMEM((stacked_rows, ROUNDS * WIDTH), jnp.float32),
            pltpu.VMEM((2, channels * ROUNDS, 128), jnp.float32),
            pltpu.VMEM((row_count, channels * ROUNDS), jnp.float32),
            pltpu.SemaphoreType.DMA((len(mates) + 1,)),
            pltpu.SemaphoreType.DMA((row_count // 128,)),
            *(pltpu.VMEM((channels, width), jnp.bfloat16) for width in widths),
        ],
        compiler_params=pltpu.CompilerParams(vmem_limit_bytes=40 * 2**20),
    )(chosen, *strain, *mates)


def pair_weights(count):
    weights, sums = [], set()
    value = 0
    while len(weights) < count:
        more = {value + weight for weight in weights}
        if not more & sums and len(more) == len(weights):
            weights.append(value)
            sums |= more
        value += 1
    return weights


def by_plan(plan, own):
    block_count = lax.axis_size("sta")
    middle = range(2, block_count - 1)
    weights = dict(zip(middle, pair_weights(len(middle))))
    choices = {weights[a] + weights[b]: (a, b) for a, b in itertools.combinations(middle, 2)}
    least = min(choices)
    index = sum(jnp.where(plan == key, weight, 0) for key, weight in weights.items())
    index = jnp.sum(index) - least

    def branch(keys):
        return lambda own: jnp.concatenate([swap(own, "sta", key) for key in keys])

    last = block_count - 1
    branches = [
        branch((1, *choices.get(total, choices[least]), last))
        for total in range(least, max(choices) + 1)
    ]
    ranks = jnp.sum((plan[None, :] < plan[:, None]).astype(jnp.int32), axis=1)
    index, ranks = lax.optimization_barrier((index, ranks))
    return ranks, lax.switch(index, branches, own)


def local(strain, plan):
    tile_count, block_count = lax.axis_size("tm"), lax.axis_size("sta")
    row_count = SOURCES * LAGS // tile_count
    here = lax.axis_index("tm")

    def source_row(tile, index):
        row = index * row_count // LAGS * (strain.shape[0] // SOURCES)
        return lax.dynamic_slice_in_dim(tile, row, 1, 0)

    even, odd = list(range(0, tile_count, 2)), list(range(1, tile_count, 2))[::-1]
    arrived = [swap(strain, "tm", key) for key in even[1:]]
    rows = [swap(source_row(strain, here ^ key), "tm", key) for key in odd]
    own = jnp.concatenate(
        rows + [source_row(strain, here)] + [source_row(tile, here) for tile in arrived], axis=1
    )
    row_order = odd + even
    tile_order = [key ^ 1 for key in even] + even
    near = jnp.concatenate([strain, *arrived])
    far = swap(near, "tm", 1)
    if ROUNDS == 4 and 5 <= block_count <= MOST_BLOCKS:
        chosen, mates = by_plan(plan, own)
        mates = [mates]
    else:
        chosen = plan
        pair = jnp.concatenate([own, swap(own, "sta", 1)])
        mates = [pair] + [swap(pair, "sta", 2 * g) for g in range(1, block_count // 2)]
    return correlate(tile_order, row_order, chosen, [far, near], mates, row_count)


def solution(mesh):
    in_specs = (P("sta", "tm"), P())
    out_specs = P("tm", "sta")
    return jax.shard_map(local, mesh=mesh, in_specs=in_specs, out_specs=out_specs, check_vma=False)
```

```python
import functools
import itertools
import math

import jax
import jax.numpy as jnp
from jax import lax
from jax.experimental import pallas as pl
from jax.experimental.pallas import tpu as pltpu
from jax.sharding import PartitionSpec as P

SOURCES = 4
MAX_LAG = 512
ROUNDS = 4
LAGS = 1024
WIDTH = 64
HALVES = 128 // WIDTH
MOST_BLOCKS = 8

epsilon = 1e-06


def swap(block, axis, key):
    count = lax.axis_size(axis)
    return lax.ppermute(block, axis, [(i, i ^ key) for i in range(count)])


def place(base, step, index):
    if isinstance(index, int):
        return base + step * index
    return pl.multiple_of(base + step * index, 128)


def stack_strain(keys, strain, stacked, wide):
    channels, tile_len = wide[0].shape[0], strain[0].shape[1]
    length = len(keys) * tile_len
    strain = [group.at[at : at + channels] for group in strain for at in range(0, group.shape[0], channels)]
    blocks = stacked.shape[0] // channels
    here = lax.axis_index("tm")
    row_count = blocks * WIDTH
    low_lag = 0 if row_count == LAGS else lax.rem(here * row_count, LAGS)

    wide[0][:, :MAX_LAG] = jnp.zeros((channels, MAX_LAG), jnp.bfloat16)
    wide[0][:, MAX_LAG + length :] = jnp.zeros((channels, MAX_LAG + 128), jnp.bfloat16)
    squares = jnp.zeros((channels, 1), jnp.float32)
    for tile in strain:
        widened = tile[...].astype(jnp.float32)
        squares += jnp.sum(widened * widened, axis=1, keepdims=True)
    scale = lax.rsqrt(squares / length + epsilon)
    for key, tile in zip(keys, strain):
        wide[0][:, pl.ds(place(MAX_LAG, tile_len, here ^ key), tile_len)] = (
            tile[...].astype(jnp.float32) * scale
        ).astype(jnp.bfloat16)
    for half in range(1, HALVES):
        kept = wide[half].shape[1]
        wide[half][...] = wide[0][:, WIDTH * half : WIDTH * half + kept]
    for j in range(blocks):
        stacked[channels * j : channels * (j + 1), :] = wide[j % HALVES][
            :, pl.ds(place(128 * (j // HALVES), 1, low_lag), stacked.shape[1])
        ]


def fill_shifts(line, shifts):
    length = line.shape[1]
    shape = (WIDTH, 128)
    mask = lax.broadcasted_iota(jnp.int32, shape, 1) >= lax.broadcasted_iota(jnp.int32, shape, 0)
    pieces = math.gcd(length // 128, 32)

    for r in range(ROUNDS):
        rows = slice(r * WIDTH, (r + 1) * WIDTH)

        def body(step, before):
            for q in range(pieces):
                at = pl.ds(place(128 * q, 128 * pieces, step), 128)
                piece = jnp.broadcast_to(line[r : r + 1, at], shape)
                now = pltpu.roll(piece, 0, 1, stride=1, stride_axis=0)
                shifts[rows, at] = jnp.where(mask, now, before).astype(jnp.bfloat16)
                before = now
            return before

        steps = length // (128 * pieces)
        zero = jnp.zeros(shape, jnp.float32)
        last = body(0, zero) if steps == 1 else lax.fori_loop(0, steps, body, zero)
        shifts[rows, length : length + 128] = jnp.where(mask, 0.0, last).astype(jnp.bfloat16)


def correlate_kernel(keys, row_keys, tiles, groups, chosen, *refs):
    strain, mates, (out, *refs) = refs[:tiles], refs[tiles : tiles + groups], refs[tiles + groups :]
    line, stacked, shifts, total, turned, ready, sent, *wide = refs
    row_count = out.shape[0]
    channels, tile_len = out.shape[1] // ROUNDS, strain[0].shape[1]
    length = line.shape[1]
    here = lax.axis_index("tm")

    for k, key in enumerate(row_keys):
        at = k * tile_len
        picked, number = jnp.zeros((ROUNDS, tile_len), jnp.float32), 0
        for group in mates:
            part = group[:, at : at + tile_len].astype(jnp.float32)
            for row in range(group.shape[0]):
                wanted = jnp.tile(chosen[...] == number, (1, tile_len // 128))
                picked = jnp.where(wanted, jnp.broadcast_to(part[row : row + 1], picked.shape), picked)
                number += 1
        line[:, pl.ds(place(0, tile_len, here ^ key), tile_len)] = picked
    stack_strain(keys, strain, stacked, wide)
    squares = jnp.sum(line[...] * line[...], axis=1, keepdims=True)
    whitened = line[...] * lax.rsqrt(squares / length + epsilon)
    line[...] = whitened.astype(jnp.bfloat16).astype(jnp.float32)
    fill_shifts(line, shifts)
    total[...] = lax.dot_general(
        stacked[...], shifts[...], (((1,), (1,)), ((), ())), preferred_element_type=jnp.float32
    )
    copies = []
    lane = lax.broadcasted_iota(jnp.int32, (channels, 128), 1)
    for block in range(row_count // 128):
        for r in range(ROUNDS):
            value = jnp.zeros((channels, 128), jnp.float32)
            for half in range(HALVES):
                rows = slice((block * HALVES + half) * channels, (block * HALVES + half + 1) * channels)
                first = WIDTH * r // 128 * 128
                part = total[rows, first : first + 128]
                if WIDTH * half != WIDTH * r - first:
                    part = pltpu.roll(part, (WIDTH * half - WIDTH * r + first) % 128, 1)
                value = part if half == 0 else jnp.where(lane >= WIDTH * half, part, value)
            turned[block % 2, pl.ds(r, channels, stride=ROUNDS), :] = value
        lags = slice(128 * block, 128 * (block + 1))
        ready[lags, :] = turned[block % 2].T * (1.0 / math.sqrt(length))
        copies.append(pltpu.make_async_copy(ready.at[lags], out.at[lags], sent.at[block]))
        copies[-1].start()
    for copy in copies:
        copy.wait()


def correlate(keys, row_keys, chosen, strain, mates, row_count):
    rows, tile_len = strain[0].shape
    channels = rows * len(strain) // len(keys)
    length = len(keys) * tile_len
    depth = length + 128
    stacked_rows = channels * row_count // WIDTH
    in_vmem = pl.BlockSpec(memory_space=pltpu.VMEM)
    widths = [length + 2 * MAX_LAG + 128] + [length + 2 * MAX_LAG] * (HALVES - 1)
    return pl.pallas_call(
        functools.partial(correlate_kernel, keys, row_keys, len(strain), len(mates)),
        out_shape=jax.ShapeDtypeStruct((row_count, channels * ROUNDS), jnp.float32),
        in_specs=[in_vmem] * (1 + len(strain) + len(mates)),
        out_specs=pl.BlockSpec(memory_space=pltpu.HBM),
        scratch_shapes=[
            pltpu.VMEM((ROUNDS, length), jnp.float32),
            pltpu.VMEM((stacked_rows, depth), jnp.bfloat16),
            pltpu.VMEM((ROUNDS * WIDTH, depth), jnp.bfloat16),
            pltpu.VMEM((stacked_rows, ROUNDS * WIDTH), jnp.float32),
            pltpu.VMEM((2, channels * ROUNDS, 128), jnp.float32),
            pltpu.VMEM((row_count, channels * ROUNDS), jnp.float32),
            pltpu.SemaphoreType.DMA((row_count // 128,)),
            *(pltpu.VMEM((channels, width), jnp.bfloat16) for width in widths),
        ],
        compiler_params=pltpu.CompilerParams(vmem_limit_bytes=40 * 2**20),
    )(chosen, *strain, *mates)


def pair_weights(count):
    weights, sums = [], set()
    value = 0
    while len(weights) < count:
        more = {value + weight for weight in weights}
        if not more & sums and len(more) == len(weights):
            weights.append(value)
            sums |= more
        value += 1
    return weights


def by_plan(plan, own):
    block_count = lax.axis_size("sta")
    middle = range(2, block_count - 1)
    weights = dict(zip(middle, pair_weights(len(middle))))
    choices = {weights[a] + weights[b]: (a, b) for a, b in itertools.combinations(middle, 2)}
    least = min(choices)
    index = sum(jnp.where(plan == key, weight, 0) for key, weight in weights.items())
    index = jnp.sum(index) - least

    def branch(keys):
        return lambda own: jnp.concatenate([swap(own, "sta", key) for key in keys])

    last = block_count - 1
    branches = [
        branch((1, *choices.get(total, choices[least]), last))
        for total in range(least, max(choices) + 1)
    ]
    ranks = jnp.sum((plan[None, :] < plan[:, None]).astype(jnp.int32), axis=1)
    ranks = jnp.broadcast_to(ranks[:, None], (ROUNDS, 128))
    index, ranks = lax.optimization_barrier((index, ranks))
    return ranks, lax.switch(index, branches, own)


def local(strain, plan):
    tile_count, block_count = lax.axis_size("tm"), lax.axis_size("sta")
    row_count = SOURCES * LAGS // tile_count
    here = lax.axis_index("tm")

    def source_row(tile, index):
        row = index * row_count // LAGS * (strain.shape[0] // SOURCES)
        return lax.dynamic_slice_in_dim(tile, row, 1, 0)

    even, odd = list(range(0, tile_count, 2)), list(range(1, tile_count, 2))[::-1]
    arrived = [swap(strain, "tm", key) for key in even[1:]]
    rows = [swap(source_row(strain, here ^ key), "tm", key) for key in odd]
    own = jnp.concatenate(
        rows + [source_row(strain, here)] + [source_row(tile, here) for tile in arrived], axis=1
    )
    row_order = odd + even
    tile_order = [key ^ 1 for key in even] + even
    near = jnp.concatenate([strain, *arrived])
    far = swap(near, "tm", 1)
    if ROUNDS == 4 and 5 <= block_count <= MOST_BLOCKS:
        chosen, mates = by_plan(plan, own)
        mates = [mates]
    else:
        chosen = jnp.broadcast_to(plan[:, None], (ROUNDS, 128))
        pair = jnp.concatenate([own, swap(own, "sta", 1)])
        mates = [pair] + [swap(pair, "sta", 2 * g) for g in range(1, block_count // 2)]
    return correlate(tile_order, row_order, chosen, [far, near], mates, row_count)


def solution(mesh):
    in_specs = (P("sta", "tm"), P())
    out_specs = P("tm", "sta")
    return jax.shard_map(local, mesh=mesh, in_specs=in_specs, out_specs=out_specs, check_vma=False)
```

```python
import functools
import itertools
import math

import jax
import jax.numpy as jnp
from jax import lax
from jax.experimental import pallas as pl
from jax.experimental.pallas import tpu as pltpu
from jax.sharding import PartitionSpec as P

SOURCES = 4
MAX_LAG = 512
ROUNDS = 4
LAGS = 1024
WIDTH = 64
HALVES = 128 // WIDTH
MOST_BLOCKS = 8

epsilon = 1e-06


def swap(block, axis, key):
    count = lax.axis_size(axis)
    return lax.ppermute(block, axis, [(i, i ^ key) for i in range(count)])


def place(base, step, index):
    if isinstance(index, int):
        return base + step * index
    return pl.multiple_of(base + step * index, 128)


def stack_strain(keys, strain, stacked, wide):
    channels, tile_len = wide[0].shape[0], strain[0].shape[1]
    length = len(keys) * tile_len
    strain = [group.at[at : at + channels] for group in strain for at in range(0, group.shape[0], channels)]
    blocks = stacked.shape[0] // channels
    here = lax.axis_index("tm")
    row_count = blocks * WIDTH
    low_lag = 0 if row_count == LAGS else lax.rem(here * row_count, LAGS)

    wide[0][:, :MAX_LAG] = jnp.zeros((channels, MAX_LAG), jnp.bfloat16)
    wide[0][:, MAX_LAG + length :] = jnp.zeros((channels, MAX_LAG + 128), jnp.bfloat16)
    squares = jnp.zeros((channels, 1), jnp.float32)
    for tile in strain:
        widened = tile[...].astype(jnp.float32)
        squares += jnp.sum(widened * widened, axis=1, keepdims=True)
    scale = lax.rsqrt(squares / length + epsilon)
    for key, tile in zip(keys, strain):
        wide[0][:, pl.ds(place(MAX_LAG, tile_len, here ^ key), tile_len)] = (
            tile[...].astype(jnp.float32) * scale
        ).astype(jnp.bfloat16)
    for half in range(1, HALVES):
        kept = wide[half].shape[1]
        wide[half][...] = wide[0][:, WIDTH * half : WIDTH * half + kept]
    for j in range(blocks):
        stacked[channels * j : channels * (j + 1), :] = wide[j % HALVES][
            :, pl.ds(place(128 * (j // HALVES), 1, low_lag), stacked.shape[1])
        ]


def fill_shifts(line, shifts):
    length = line.shape[1]
    shape = (WIDTH, 128)
    mask = lax.broadcasted_iota(jnp.int32, shape, 1) >= lax.broadcasted_iota(jnp.int32, shape, 0)
    pieces = math.gcd(length // 128, 32)

    for r in range(ROUNDS):
        rows = slice(r * WIDTH, (r + 1) * WIDTH)

        def body(step, before):
            for q in range(pieces):
                at = pl.ds(place(128 * q, 128 * pieces, step), 128)
                piece = jnp.broadcast_to(line[r : r + 1, at], shape)
                now = pltpu.roll(piece, 0, 1, stride=1, stride_axis=0)
                shifts[rows, at] = jnp.where(mask, now, before).astype(jnp.bfloat16)
                before = now
            return before

        steps = length // (128 * pieces)
        zero = jnp.zeros(shape, jnp.float32)
        last = body(0, zero) if steps == 1 else lax.fori_loop(0, steps, body, zero)
        shifts[rows, length : length + 128] = jnp.where(mask, 0.0, last).astype(jnp.bfloat16)


def correlate_kernel(keys, row_keys, tiles, groups, chosen, *refs):
    strain, mates, (out, *refs) = refs[:tiles], refs[tiles : tiles + groups], refs[tiles + groups :]
    line, stacked, shifts, total, turned, ready, sent, *wide = refs
    row_count = out.shape[0]
    channels, tile_len = out.shape[1] // ROUNDS, strain[0].shape[1]
    length = line.shape[1]
    here = lax.axis_index("tm")

    for k, key in enumerate(row_keys):
        at = k * tile_len
        picked, number = jnp.zeros((ROUNDS, tile_len), jnp.float32), 0
        for group in mates:
            part = group[:, at : at + tile_len].astype(jnp.float32)
            for row in range(group.shape[0]):
                wanted = jnp.tile(chosen[...] == number, (1, tile_len // 128))
                picked = jnp.where(wanted, jnp.broadcast_to(part[row : row + 1], picked.shape), picked)
                number += 1
        line[:, pl.ds(place(0, tile_len, here ^ key), tile_len)] = picked
    stack_strain(keys, strain, stacked, wide)
    squares = jnp.sum(line[...] * line[...], axis=1, keepdims=True)
    whitened = line[...] * lax.rsqrt(squares / length + epsilon)
    line[...] = whitened.astype(jnp.bfloat16).astype(jnp.float32)
    fill_shifts(line, shifts)
    total[...] = lax.dot_general(
        stacked[...], shifts[...], (((1,), (1,)), ((), ())), preferred_element_type=jnp.float32
    )
    copies = []
    lane = lax.broadcasted_iota(jnp.int32, (channels, 128), 1)
    for block in range(row_count // 128):
        for r in range(ROUNDS):
            value = jnp.zeros((channels, 128), jnp.float32)
            for half in range(HALVES):
                rows = slice((block * HALVES + half) * channels, (block * HALVES + half + 1) * channels)
                first = WIDTH * r // 128 * 128
                part = total[rows, first : first + 128]
                if WIDTH * half != WIDTH * r - first:
                    part = pltpu.roll(part, (WIDTH * half - WIDTH * r + first) % 128, 1)
                value = part if half == 0 else jnp.where(lane >= WIDTH * half, part, value)
            turned[block % 2, pl.ds(r, channels, stride=ROUNDS), :] = value
        lags = slice(128 * block, 128 * (block + 1))
        ready[lags, :] = turned[block % 2].T * (1.0 / math.sqrt(length))
        copies.append(pltpu.make_async_copy(ready.at[lags], out.at[lags], sent.at[block]))
        copies[-1].start()
    for copy in copies:
        copy.wait()


def correlate(keys, row_keys, chosen, strain, mates, row_count):
    rows, tile_len = strain[0].shape
    channels = rows * len(strain) // len(keys)
    length = len(keys) * tile_len
    depth = length + 128
    stacked_rows = channels * row_count // WIDTH
    in_vmem = pl.BlockSpec(memory_space=pltpu.VMEM)
    widths = [length + 2 * MAX_LAG + 128] + [length + 2 * MAX_LAG] * (HALVES - 1)
    return pl.pallas_call(
        functools.partial(correlate_kernel, keys, row_keys, len(strain), len(mates)),
        out_shape=jax.ShapeDtypeStruct((row_count, channels * ROUNDS), jnp.float32),
        in_specs=[in_vmem] * (1 + len(strain) + len(mates)),
        out_specs=pl.BlockSpec(memory_space=pltpu.HBM),
        scratch_shapes=[
            pltpu.VMEM((ROUNDS, length), jnp.float32),
            pltpu.VMEM((stacked_rows, depth), jnp.bfloat16),
            pltpu.VMEM((ROUNDS * WIDTH, depth), jnp.bfloat16),
            pltpu.VMEM((stacked_rows, ROUNDS * WIDTH), jnp.float32),
            pltpu.VMEM((2, channels * ROUNDS, 128), jnp.float32),
            pltpu.VMEM((row_count, channels * ROUNDS), jnp.float32),
            pltpu.SemaphoreType.DMA((row_count // 128,)),
            *(pltpu.VMEM((channels, width), jnp.bfloat16) for width in widths),
        ],
        compiler_params=pltpu.CompilerParams(vmem_limit_bytes=40 * 2**20),
    )(chosen, *strain, *mates)


def pair_weights(count):
    weights, sums = [], set()
    value = 0
    while len(weights) < count:
        more = {value + weight for weight in weights}
        if not more & sums and len(more) == len(weights):
            weights.append(value)
            sums |= more
        value += 1
    return weights


def by_plan(plan, own):
    block_count = lax.axis_size("sta")
    middle = range(2, block_count - 1)
    weights = dict(zip(middle, pair_weights(len(middle))))
    choices = {weights[a] + weights[b]: (a, b) for a, b in itertools.combinations(middle, 2)}
    least = min(choices)
    index = sum(jnp.where(plan == key, weight, 0) for key, weight in weights.items())
    index = jnp.sum(index) - least

    def branch(keys):
        return lambda own: jnp.concatenate([swap(own, "sta", key) for key in keys])

    last = block_count - 1

    def turn(key):
        even, final = 1 - (key & 1), key == last
        return key + even * 2 * (block_count - key) + final * 2 * block_count

    branches = [
        branch(sorted((1, *choices.get(total, choices[least]), last), key=turn))
        for total in range(least, max(choices) + 1)
    ]
    turns = turn(plan)
    ranks = jnp.sum((turns[None, :] < turns[:, None]).astype(jnp.int32), axis=1)
    ranks = jnp.broadcast_to(ranks[:, None], (ROUNDS, 128))
    index, ranks = lax.optimization_barrier((index, ranks))
    return ranks, lax.switch(index, branches, own)


def local(strain, plan):
    tile_count, block_count = lax.axis_size("tm"), lax.axis_size("sta")
    row_count = SOURCES * LAGS // tile_count
    here = lax.axis_index("tm")

    def source_row(tile, index):
        row = index * row_count // LAGS * (strain.shape[0] // SOURCES)
        return lax.dynamic_slice_in_dim(tile, row, 1, 0)

    even, odd = list(range(0, tile_count, 2)), list(range(1, tile_count, 2))[::-1]
    arrived = [swap(strain, "tm", key) for key in even[1:]]
    rows = [swap(source_row(strain, here ^ key), "tm", key) for key in odd]
    own = jnp.concatenate(
        rows + [source_row(strain, here)] + [source_row(tile, here) for tile in arrived], axis=1
    )
    row_order = odd + even
    tile_order = [key ^ 1 for key in even] + even
    near = jnp.concatenate([strain, *arrived])
    far = swap(near, "tm", 1)
    if ROUNDS == 4 and 5 <= block_count <= MOST_BLOCKS:
        chosen, mates = by_plan(plan, own)
        mates = [mates]
    else:
        chosen = jnp.broadcast_to(plan[:, None], (ROUNDS, 128))
        pair = jnp.concatenate([own, swap(own, "sta", 1)])
        mates = [pair] + [swap(pair, "sta", 2 * g) for g in range(1, block_count // 2)]
    return correlate(tile_order, row_order, chosen, [far, near], mates, row_count)


def solution(mesh):
    in_specs = (P("sta", "tm"), P())
    out_specs = P("tm", "sta")
    return jax.shard_map(local, mesh=mesh, in_specs=in_specs, out_specs=out_specs, check_vma=False)
```

```python
import functools
import itertools
import math

import jax
import jax.numpy as jnp
from jax import lax
from jax.experimental import pallas as pl
from jax.experimental.pallas import tpu as pltpu
from jax.sharding import PartitionSpec as P

SOURCES = 4
MAX_LAG = 512
ROUNDS = 4
LAGS = 1024
WIDTH = 64
HALVES = 128 // WIDTH
MOST_BLOCKS = 8

epsilon = 1e-06


def swap(block, axis, key):
    count = lax.axis_size(axis)
    return lax.ppermute(block, axis, [(i, i ^ key) for i in range(count)])


def place(base, step, index):
    if isinstance(index, int):
        return base + step * index
    return pl.multiple_of(base + step * index, 128)


def stack_strain(keys, strain, stacked, wide):
    channels, tile_len = wide[0].shape[0], strain[0].shape[1]
    length = len(keys) * tile_len
    strain = [group.at[at : at + channels] for group in strain for at in range(0, group.shape[0], channels)]
    blocks = stacked.shape[0] // channels
    here = lax.axis_index("tm")
    row_count = blocks * WIDTH
    low_lag = 0 if row_count == LAGS else lax.rem(here * row_count, LAGS)

    wide[0][:, :MAX_LAG] = jnp.zeros((channels, MAX_LAG), jnp.bfloat16)
    wide[0][:, MAX_LAG + length :] = jnp.zeros((channels, MAX_LAG + 128), jnp.bfloat16)
    squares = jnp.zeros((channels, 1), jnp.float32)
    for tile in strain:
        widened = tile[...].astype(jnp.float32)
        squares += jnp.sum(widened * widened, axis=1, keepdims=True)
    scale = lax.rsqrt(squares / length + epsilon)
    for key, tile in zip(keys, strain):
        wide[0][:, pl.ds(place(MAX_LAG, tile_len, here ^ key), tile_len)] = (
            tile[...].astype(jnp.float32) * scale
        ).astype(jnp.bfloat16)
    for half in range(1, HALVES):
        kept = wide[half].shape[1]
        wide[half][...] = wide[0][:, WIDTH * half : WIDTH * half + kept]
    for j in range(blocks):
        stacked[channels * j : channels * (j + 1), :] = wide[j % HALVES][
            :, pl.ds(place(128 * (j // HALVES), 1, low_lag), stacked.shape[1])
        ]


def fill_shifts(line, shifts):
    length = line.shape[1]
    shape = (WIDTH, 128)
    mask = lax.broadcasted_iota(jnp.int32, shape, 1) >= lax.broadcasted_iota(jnp.int32, shape, 0)
    pieces = math.gcd(length // 128, 32)

    for r in range(ROUNDS):
        rows = slice(r * WIDTH, (r + 1) * WIDTH)

        def body(step, before):
            for q in range(pieces):
                at = pl.ds(place(128 * q, 128 * pieces, step), 128)
                piece = jnp.broadcast_to(line[r : r + 1, at], shape)
                now = pltpu.roll(piece, 0, 1, stride=1, stride_axis=0)
                shifts[rows, at] = jnp.where(mask, now, before).astype(jnp.bfloat16)
                before = now
            return before

        steps = length // (128 * pieces)
        zero = jnp.zeros(shape, jnp.float32)
        last = body(0, zero) if steps == 1 else lax.fori_loop(0, steps, body, zero)
        shifts[rows, length : length + 128] = jnp.where(mask, 0.0, last).astype(jnp.bfloat16)


def correlate_kernel(keys, row_keys, ranked, tiles, groups, chosen, *refs):
    strain, mates, (out, *refs) = refs[:tiles], refs[tiles : tiles + groups], refs[tiles + groups :]
    line, stacked, shifts, total, turned, ready, sent, *wide = refs
    row_count = out.shape[0]
    channels, tile_len = out.shape[1] // ROUNDS, strain[0].shape[1]
    length = line.shape[1]
    here = lax.axis_index("tm")

    number_of = chosen[...]
    if ranked:
        even = jnp.where(number_of % 2 == 0, 2 * (ranked - number_of), 0)
        turns = number_of + even + jnp.where(number_of == ranked - 1, 2 * ranked, 0)
        number_of = jnp.zeros_like(turns)
        for r in range(ROUNDS):
            number_of += jnp.where(jnp.broadcast_to(turns[r : r + 1], turns.shape) < turns, 1, 0)
    for k, key in enumerate(row_keys):
        at = k * tile_len
        picked, number = jnp.zeros((ROUNDS, tile_len), jnp.float32), 0
        for group in mates:
            part = group[:, at : at + tile_len].astype(jnp.float32)
            for row in range(group.shape[0]):
                wanted = jnp.tile(number_of == number, (1, tile_len // 128))
                picked = jnp.where(wanted, jnp.broadcast_to(part[row : row + 1], picked.shape), picked)
                number += 1
        line[:, pl.ds(place(0, tile_len, here ^ key), tile_len)] = picked
    stack_strain(keys, strain, stacked, wide)
    squares = jnp.sum(line[...] * line[...], axis=1, keepdims=True)
    whitened = line[...] * lax.rsqrt(squares / length + epsilon)
    line[...] = whitened.astype(jnp.bfloat16).astype(jnp.float32)
    fill_shifts(line, shifts)
    total[...] = lax.dot_general(
        stacked[...], shifts[...], (((1,), (1,)), ((), ())), preferred_element_type=jnp.float32
    )
    copies = []
    lane = lax.broadcasted_iota(jnp.int32, (channels, 128), 1)
    for block in range(row_count // 128):
        for r in range(ROUNDS):
            value = jnp.zeros((channels, 128), jnp.float32)
            for half in range(HALVES):
                rows = slice((block * HALVES + half) * channels, (block * HALVES + half + 1) * channels)
                first = WIDTH * r // 128 * 128
                part = total[rows, first : first + 128]
                if WIDTH * half != WIDTH * r - first:
                    part = pltpu.roll(part, (WIDTH * half - WIDTH * r + first) % 128, 1)
                value = part if half == 0 else jnp.where(lane >= WIDTH * half, part, value)
            turned[block % 2, pl.ds(r, channels, stride=ROUNDS), :] = value
        lags = slice(128 * block, 128 * (block + 1))
        ready[lags, :] = turned[block % 2].T * (1.0 / math.sqrt(length))
        copies.append(pltpu.make_async_copy(ready.at[lags], out.at[lags], sent.at[block]))
        copies[-1].start()
    for copy in copies:
        copy.wait()


def correlate(keys, row_keys, ranked, chosen, strain, mates, row_count):
    rows, tile_len = strain[0].shape
    channels = rows * len(strain) // len(keys)
    length = len(keys) * tile_len
    depth = length + 128
    stacked_rows = channels * row_count // WIDTH
    in_vmem = pl.BlockSpec(memory_space=pltpu.VMEM)
    widths = [length + 2 * MAX_LAG + 128] + [length + 2 * MAX_LAG] * (HALVES - 1)
    return pl.pallas_call(
        functools.partial(correlate_kernel, keys, row_keys, ranked, len(strain), len(mates)),
        out_shape=jax.ShapeDtypeStruct((row_count, channels * ROUNDS), jnp.float32),
        in_specs=[in_vmem] * (1 + len(strain) + len(mates)),
        out_specs=pl.BlockSpec(memory_space=pltpu.HBM),
        scratch_shapes=[
            pltpu.VMEM((ROUNDS, length), jnp.float32),
            pltpu.VMEM((stacked_rows, depth), jnp.bfloat16),
            pltpu.VMEM((ROUNDS * WIDTH, depth), jnp.bfloat16),
            pltpu.VMEM((stacked_rows, ROUNDS * WIDTH), jnp.float32),
            pltpu.VMEM((2, channels * ROUNDS, 128), jnp.float32),
            pltpu.VMEM((row_count, channels * ROUNDS), jnp.float32),
            pltpu.SemaphoreType.DMA((row_count // 128,)),
            *(pltpu.VMEM((channels, width), jnp.bfloat16) for width in widths),
        ],
        compiler_params=pltpu.CompilerParams(vmem_limit_bytes=40 * 2**20),
    )(chosen, *strain, *mates)


def turn_of(key, block_count):
    even = 1 - (key & 1)
    final = (key == block_count - 1) * 2
    return key + even * 2 * (block_count - key) + final * block_count


def pair_weights(count):
    weights, sums = [], set()
    value = 0
    while len(weights) < count:
        more = {value + weight for weight in weights}
        if not more & sums and len(more) == len(weights):
            weights.append(value)
            sums |= more
        value += 1
    return weights


def by_plan(plan, own):
    block_count = lax.axis_size("sta")
    middle = range(2, block_count - 1)
    weights = dict(zip(middle, pair_weights(len(middle))))
    choices = {weights[a] + weights[b]: (a, b) for a, b in itertools.combinations(middle, 2)}
    least = min(choices)
    index = sum(jnp.where(plan == key, weight, 0) for key, weight in weights.items())
    index = jnp.sum(index) - least

    def branch(keys):
        return lambda own: jnp.concatenate([swap(own, "sta", key) for key in keys])

    last = block_count - 1

    branches = [
        branch(sorted((1, *choices.get(total, choices[least]), last), key=lambda key: turn_of(key, block_count)))
        for total in range(least, max(choices) + 1)
    ]
    ranks = jnp.broadcast_to(plan[:, None], (ROUNDS, 128))
    index, ranks = lax.optimization_barrier((index, ranks))
    return ranks, lax.switch(index, branches, own)


def local(strain, plan):
    tile_count, block_count = lax.axis_size("tm"), lax.axis_size("sta")
    row_count = SOURCES * LAGS // tile_count
    here = lax.axis_index("tm")

    def source_row(tile, index):
        row = index * row_count // LAGS * (strain.shape[0] // SOURCES)
        return lax.dynamic_slice_in_dim(tile, row, 1, 0)

    even, odd = list(range(0, tile_count, 2)), list(range(1, tile_count, 2))[::-1]
    arrived = [swap(strain, "tm", key) for key in even[1:]]
    rows = [swap(source_row(strain, here ^ key), "tm", key) for key in odd]
    own = jnp.concatenate(
        rows + [source_row(strain, here)] + [source_row(tile, here) for tile in arrived], axis=1
    )
    row_order = odd + even
    tile_order = [key ^ 1 for key in even] + even
    near = jnp.concatenate([strain, *arrived])
    far = swap(near, "tm", 1)
    if ROUNDS == 4 and 5 <= block_count <= MOST_BLOCKS:
        chosen, mates = by_plan(plan, own)
        mates, ranked = [mates], block_count
    else:
        chosen, ranked = jnp.broadcast_to(plan[:, None], (ROUNDS, 128)), 0
        pair = jnp.concatenate([own, swap(own, "sta", 1)])
        mates = [pair] + [swap(pair, "sta", 2 * g) for g in range(1, block_count // 2)]
    return correlate(tile_order, row_order, ranked, chosen, [far, near], mates, row_count)


def solution(mesh):
    in_specs = (P("sta", "tm"), P())
    out_specs = P("tm", "sta")
    return jax.shard_map(local, mesh=mesh, in_specs=in_specs, out_specs=out_specs, check_vma=False)
```
